32 devices in a mesh: seq: 32 (over z, y, x, core), head: 1.
Axes of the slice: x: 2, y: 2, z: 4, core: 2. Of those that a mesh axis runs over, the one named last changes fastest.
Arguments:
- query_rows: bfloat16 [4096, 2048], P('seq', 'head'), may hold values from -6 to 6
- key_rows: bfloat16 [4096, 2048], P('seq', 'head'), may hold values from -6 to 6
- value_rows: bfloat16 [4096, 2048], P('seq', 'head'), may hold values from -6 to 6
- doc_lengths: int32 [32], replicated, may hold values from 1 to 1920, 4096 in all
- norm_gain: float32 [128], replicated, may hold values from 0.25 to 1.75
- out_weight: bfloat16 [2048, 2048], P('head'), may hold values from -0.125 to 0.125
Outputs:
- layer_out: bfloat16 [4096, 2048], P('seq', 'head')
The draws below stay inside these ranges and needn't reach their ends.
Inputs may be any that keep to these rules, and one draw needn't show every extreme that they name: `doc_lengths`: positive lengths summing to 4096; the longest has exactly 1920 tokens.
All inputs are finite; a program needn't handle non-finite values.
Results may differ from the reference program's by a relative error of at most 0.0049.
Values sent between devices are 32-bit elements; how exact they have to be, the bound alone decides.
No kernel may reach another device: no remote copies, remote signals or barrier semaphores. Data moves between devices by JAX's collectives and lax.ppermute only.
A program may use at most 320 MiB of HBM per device.

```python
import math
import jax
import jax.numpy as jnp
import numpy as np
from jax import lax

HEADS = 16
HEAD_DIM = 128
TOK_DEV = 128
ITERS = 4
D = 2048
TOKENS = 4096
DOCS = 32
MOST = 1920


def levels(key, dims, split, smallest, top_value):
    def one(position, shards_of):
        draws = jax.random.uniform(jax.random.fold_in(jax.random.fold_in(key, 6), position), (shards_of,), jnp.float32, smallest / len(split), top_value / len(split))
        return jnp.repeat(jnp.exp(draws), dims[position] // shards_of).reshape((-1,) + (1,) * (len(dims) - position - 1))

    level = one(*split[0])
    for cut in split[1:]:
        level = level * one(*cut)
    return level


def profile(count, total, limit, lean):
    weights = [(1 << 20) // math.isqrt(standing ** lean) + 1 for standing in range(2, count + 1)]
    spare, holding = total - limit - (count - 1), [1] * (count - 1)
    while spare > 0:
        free = [i for i in range(count - 1) if holding[i] < limit]
        mass, budget = sum([weights[i] for i in free]), spare
        for i in free:
            addition = min(limit - holding[i], max(1, budget * weights[i] // mass), spare)
            holding[i] = holding[i] + addition
            spare = spare - addition
    return np.array([limit] + holding)


def ragged_sizes(stream_key, number_of, total, reach, lean):
    if number_of == 2:
        one = jax.random.randint(stream_key, (), max(1, total - reach), min(reach, total - 1) + 1)
        return jnp.stack([one, total - one])
    tallies = jnp.asarray(profile(number_of, total, reach, lean), jnp.int32)
    couples = (number_of - 1) // 2
    giver, receiver = tallies[1:1 + 2 * couples:2], tallies[2:2 + 2 * couples:2]
    room = jnp.minimum(giver - 1, reach - receiver)
    passed = jax.random.randint(jax.random.fold_in(stream_key, 1), (couples,), 0, 1 << 20) % (room + 1)
    tallies = tallies.at[1:1 + 2 * couples:2].set(giver - passed).at[2:2 + 2 * couples:2].set(receiver + passed)
    return tallies[jax.random.permutation(jax.random.fold_in(stream_key, 2), number_of)]


def normal_values(rng, extent, scale, most, split=(), kind=jnp.bfloat16):
    result = jax.random.normal(rng, extent, jnp.float32) * scale
    if len(split) > 0:
        result = levels(rng, extent, split, -0.22, 0.18) * result
    return jnp.clip(result, min=-most, max=most).astype(kind)


def setup_inputs(seed: int = 0) -> dict:
    keys = jax.random.split(jax.random.key(seed), 7)
    return {
        "query_rows": normal_values(keys[0], (TOKENS, D), 1.0, 6.0, ((0, 32),)),
        "key_rows": normal_values(keys[1], (TOKENS, D), 1.0, 6.0, ((0, 32),)),
        "value_rows": normal_values(keys[2], (TOKENS, D), 1.0, 6.0, ((0, 32),)),
        "doc_lengths": ragged_sizes(keys[3], DOCS, TOKENS, MOST, 2).astype(jnp.int32),
        "norm_gain": jnp.clip(1.0 + 0.15 * jax.random.normal(keys[4], (HEAD_DIM,), jnp.float32), 0.25, 1.75),
        "out_weight": normal_values(keys[5], (D, D), D ** -0.5, 0.125),
    }


epsilon = 1e-06
damping = 1.0
highest = lax.Precision.HIGHEST

def unit_rows(matrix_rows):
    matrix_rows = matrix_rows.astype(jnp.float32)
    return matrix_rows * lax.rsqrt(lax.optimization_barrier(jnp.sum(matrix_rows * matrix_rows, axis=-1, keepdims=True)) + epsilon)

def document_ids(doc_lengths, positions):
    starts = jnp.cumsum(doc_lengths, dtype=jnp.int32) - doc_lengths
    below = (starts[None, :] <= positions[:, None]).astype(jnp.int32)
    return lax.optimization_barrier(jnp.sum(below, axis=1, dtype=jnp.int32)) - 1

def apply_state(vector, prefix_state, carried, mask, key_block, target):
    from_prefix = jnp.einsum('htj,hij->hti', vector, prefix_state, precision=highest) * carried[None, :, None]
    scores = jnp.einsum('htj,hsj->hts', vector, key_block, precision=highest) * mask[None]
    return from_prefix + jnp.einsum('hts,hsi->hti', scores, target, precision=highest)

def solve_block(queries, key_block, value_block, gram, cross, carried, mask):
    solution = jnp.zeros_like(queries)
    residual = queries
    direction = queries
    norm_now = lax.optimization_barrier(jnp.sum(residual * residual, axis=-1, keepdims=True))
    for iteration in range(ITERS):
        product_image = apply_state(direction, gram, carried, mask, key_block, key_block) + damping * direction
        step_size = norm_now / (lax.optimization_barrier(jnp.sum(direction * product_image, axis=-1, keepdims=True)) + epsilon)
        solution = solution + step_size * direction
        residual = residual - step_size * product_image
        norm_next = lax.optimization_barrier(jnp.sum(residual * residual, axis=-1, keepdims=True))
        direction = residual + norm_next / (norm_now + epsilon) * direction
        norm_now = norm_next
    return apply_state(solution, cross, carried, mask, key_block, value_block)

def tail_states(key_block, value_block, tail_mask):
    gram = jnp.einsum('hsi,hsj->hij', key_block * tail_mask[None, :, None], key_block, precision=highest)
    cross = jnp.einsum('hsi,hsj->hij', value_block * tail_mask[None, :, None], key_block, precision=highest)
    return (gram, cross)

def reference(query_rows, key_rows, value_rows, doc_lengths, norm_gain, out_weight):
    blocks = TOKENS // TOK_DEV

    def heads_first(matrix_rows):
        return matrix_rows.reshape(blocks, TOK_DEV, HEADS, HEAD_DIM).transpose(0, 2, 1, 3)
    queries = unit_rows(heads_first(query_rows))
    keys_all = unit_rows(heads_first(key_rows))
    values = heads_first(value_rows).astype(jnp.float32)
    positions = jnp.arange(TOKENS, dtype=jnp.int32)
    doc_ids = document_ids(doc_lengths, positions).reshape(blocks, TOK_DEV)
    offsets = jnp.arange(TOK_DEV, dtype=jnp.int32)
    causal = offsets[None, :] <= offsets[:, None]

    def advance(carried_state, inputs):
        gram, cross, previous = carried_state
        query_block, key_block, value_block, block_ids = inputs
        carried = (block_ids == previous).astype(jnp.float32)
        mask = ((block_ids[:, None] == block_ids[None, :]) & causal).astype(jnp.float32)
        mixed_heads = solve_block(query_block, key_block, value_block, gram, cross, carried, mask)
        tail_mask = (block_ids == block_ids[-1]).astype(jnp.float32)
        carry_on = (block_ids[-1] == previous).astype(jnp.float32)
        tail_gram, tail_cross = tail_states(key_block, value_block, tail_mask)
        return ((tail_gram + carry_on * gram, tail_cross + carry_on * cross, block_ids[-1]), mixed_heads)
    initial = (jnp.zeros((HEADS, HEAD_DIM, HEAD_DIM), jnp.float32), jnp.zeros((HEADS, HEAD_DIM, HEAD_DIM), jnp.float32), jnp.int32(-1))
    unused, mixed_heads = lax.scan(advance, initial, (queries, keys_all, values, doc_ids))
    inverse_rms = lax.rsqrt(lax.optimization_barrier(jnp.mean(mixed_heads * mixed_heads, axis=-1, keepdims=True)) + epsilon)
    normed = (mixed_heads * inverse_rms * norm_gain).astype(jnp.bfloat16)
    normed = normed.transpose(0, 2, 1, 3).reshape(TOKENS, D)
    return jnp.dot(normed, out_weight, preferred_element_type=jnp.float32).astype(jnp.bfloat16)
```

```python
import math

import jax
import jax.numpy as jnp
from jax import lax
from jax.sharding import PartitionSpec as P

HEAD_DIM = 128
ITERS = 4
GROUP = 16


epsilon = 1e-06
damping = 1.0
highest = lax.Precision.HIGHEST


def shifted(block, axis, distance):
    devices = range(lax.axis_size(axis))
    route = [(i - distance, i) for i in devices if i - distance in devices]
    return lax.ppermute(block, axis, route)


def unit_rows(matrix_rows):
    matrix_rows = matrix_rows.astype(jnp.float32)
    return matrix_rows * lax.rsqrt(
        jnp.sum(matrix_rows * matrix_rows, axis=-1, keepdims=True) + epsilon
    )


def document_ids(doc_lengths, positions):
    starts = jnp.cumsum(doc_lengths, dtype=jnp.int32) - doc_lengths
    below = (starts[None, :] <= positions[:, None]).astype(jnp.int32)
    return jnp.sum(below, axis=1, dtype=jnp.int32) - 1


def apply_state(vector, prefix_state, carried, mask, key_block, target):
    from_prefix = (
        jnp.einsum("htj,hij->hti", vector, prefix_state, precision=highest) * carried[None, :, None]
    )
    scores = jnp.einsum("htj,hsj->hts", vector, key_block, precision=highest) * mask[None]
    return from_prefix + jnp.einsum("hts,hsi->hti", scores, target, precision=highest)


def solve_block(queries, key_block, value_block, gram, cross, carried, mask):
    solution = jnp.zeros_like(queries)
    residual = queries
    direction = queries
    norm_now = jnp.sum(residual * residual, axis=-1, keepdims=True)
    for iteration in range(ITERS):
        product_image = (
            apply_state(direction, gram, carried, mask, key_block, key_block) + damping * direction
        )
        step_size = norm_now / (
            jnp.sum(direction * product_image, axis=-1, keepdims=True) + epsilon
        )
        solution = solution + step_size * direction
        residual = residual - step_size * product_image
        norm_next = jnp.sum(residual * residual, axis=-1, keepdims=True)
        direction = residual + norm_next / (norm_now + epsilon) * direction
        norm_now = norm_next
    return apply_state(solution, cross, carried, mask, key_block, value_block)


def on_device(query_rows, key_rows, value_rows, doc_lengths, norm_gain, out_weight):
    tokens_here = query_rows.shape[0]
    heads_here = query_rows.shape[1] // HEAD_DIM

    def heads_first(matrix_rows):
        return matrix_rows.reshape(tokens_here, heads_here, HEAD_DIM).transpose(1, 0, 2)

    queries = unit_rows(heads_first(query_rows))
    keys_here = unit_rows(heads_first(key_rows))
    values = heads_first(value_rows).astype(jnp.float32)
    shard_index = lax.axis_index("seq")
    offsets = jnp.arange(tokens_here, dtype=jnp.int32)
    positions = shard_index * tokens_here + offsets
    doc_ids = document_ids(doc_lengths, positions)
    previous = document_ids(doc_lengths, positions[:1] - 1)[0]
    carried = (doc_ids == previous).astype(jnp.float32)
    tail_mask = (doc_ids == doc_ids[-1]).astype(jnp.float32)
    tail_gram = jnp.einsum(
        "hsi,hsj->hij", keys_here * tail_mask[None, :, None], keys_here, precision=highest
    )
    tail_cross = jnp.einsum(
        "hsi,hsj->hij", values * tail_mask[None, :, None], keys_here, precision=highest
    )
    size = lax.axis_size("seq")
    group = math.gcd(size, GROUP)
    groups = [list(range(first, first + group)) for first in range(0, size, group)]
    first = shard_index // group * group
    bounds = (first + jnp.arange(group + 1, dtype=jnp.int32)) * tokens_here - 1
    before = document_ids(doc_lengths, bounds)
    goes_on = (before[1:] == before[:-1]).astype(jnp.float32)
    tails = jnp.concatenate([tail_gram, tail_cross], axis=1)
    pieces = tails.reshape(group, heads_here * 2 * HEAD_DIM // group, HEAD_DIM)
    pieces = lax.all_to_all(pieces, "seq", 0, 0, axis_index_groups=groups, tiled=True)
    running = jnp.zeros_like(pieces[0])
    through = jnp.float32(1)
    prefixes, throughs = [], []
    for j in range(group):
        prefixes.append(running)
        throughs.append(through)
        running = pieces[j] + goes_on[j] * running
        through = through * goes_on[j]
    carry = shifted(running, "seq", group)
    prefixes = jnp.stack([p + t * carry for p, t in zip(prefixes, throughs)])
    prefixes = lax.all_to_all(prefixes, "seq", 0, 0, axis_index_groups=groups, tiled=True)
    states = prefixes.reshape(heads_here, 2 * HEAD_DIM, HEAD_DIM)
    gram, cross = states[:, :HEAD_DIM], states[:, HEAD_DIM:]
    causal = offsets[None, :] <= offsets[:, None]
    mask = ((doc_ids[:, None] == doc_ids[None, :]) & causal).astype(jnp.float32)
    mixed_heads = solve_block(queries, keys_here, values, gram, cross, carried, mask)
    inverse_rms = lax.rsqrt(jnp.mean(mixed_heads * mixed_heads, axis=-1, keepdims=True) + epsilon)
    normed = (mixed_heads * inverse_rms * norm_gain).astype(jnp.bfloat16)
    normed = normed.transpose(1, 0, 2).reshape(tokens_here, heads_here * HEAD_DIM)
    partial_out = jnp.dot(normed, out_weight, preferred_element_type=jnp.float32)
    return lax.psum_scatter(partial_out, "head", scatter_dimension=1, tiled=True).astype(
        jnp.bfloat16
    )


def solution(mesh):
    in_specs = (P("seq", "head"), P("seq", "head"), P("seq", "head"), P(), P(), P("head", None))
    out_specs = P("seq", "head")
    return jax.shard_map(
        on_device, mesh=mesh, in_specs=in_specs, out_specs=out_specs, check_vma=False
    )
```
